32 devices in a mesh: row: 2 (over core), col: 16 (over z, y, x).
Axes of the slice: x: 2, y: 2, z: 4, core: 2. Of those that a mesh axis runs over, the one named last changes fastest.
Arguments:
- basis_out: float32 [16384, 16384], P('row', 'col'), may hold values from -0.046875 to 0.046875
- basis_in: float32 [16384, 16384], P('col', 'row'), may hold values from -0.046875 to 0.046875
- eig_damped: float32 [16384, 16384], P('col', 'row'), may hold values from 0.5 to 8
- query_left: bfloat16 [16384, 256], P(('row', 'col')), may hold values from -0.375 to 0.375
- query_right: bfloat16 [16384, 256], P('col'), may hold values from -6 to 6
- train_left: bfloat16 [16384, 512], P(('row', 'col')), may hold values from -0.046875 to 0.046875
- train_right: bfloat16 [16384, 512], P('col'), may hold values from -0.046875 to 0.046875
Outputs:
- response: float32 [16384, 512], P(('row', 'col'))
- scores: float32 [512], replicated
The draws below stay inside these ranges and needn't reach their ends.
All inputs are finite; a program needn't handle non-finite values.
Results may differ from the reference program's by a relative error of at most 0.0003.
Values may be sent and summed in bfloat16 or wider, within the bound.
A program may use at most 256 MiB of HBM per device.

```python
import math
import jax
import jax.numpy as jnp
from jax import lax

D_OUT = 16384
D_IN = 16384
RANK = 256
TRAIN = 512


def block_levels(key, dims, shards, least, largest):
    def one(position, shards_of):
        heights = jax.random.uniform(jax.random.fold_in(jax.random.fold_in(key, 6), position), (shards_of,), jnp.float32, least / len(shards), largest / len(shards))
        return jnp.repeat(jnp.exp(heights), dims[position] // shards_of).reshape((-1,) + (1,) * (len(dims) - position - 1))

    loudness = one(*shards[0])
    for cut in shards[1:]:
        loudness = loudness * one(*cut)
    return loudness


def bell_draw(stream_key, shape, deviation, bound, pieces=(), held_as=jnp.bfloat16):
    values = jax.random.normal(stream_key, shape, jnp.float32) * deviation
    if len(pieces) > 0:
        values = block_levels(stream_key, shape, pieces, -0.22, 0.18) * values
    return jnp.clip(values, min=-bound, max=bound).astype(held_as)


def setup_inputs(seed: int = 0) -> dict:
    arg_keys = jax.random.split(jax.random.key(seed), 8)
    return {
        "basis_out": bell_draw(arg_keys[0], (D_OUT, D_OUT), D_OUT ** -0.5, 0.046875, ((0, 2), (1, 16)), jnp.float32),
        "basis_in": bell_draw(arg_keys[1], (D_IN, D_IN), D_IN ** -0.5, 0.046875, ((0, 16), (1, 2)), jnp.float32),
        "eig_damped": jnp.clip(jnp.exp(math.log(8.0) - 2.7725887 * jax.random.uniform(arg_keys[2], (D_OUT, D_IN), jnp.float32) ** block_levels(arg_keys[2], (D_OUT, D_IN), ((0, 16), (1, 2)), -0.2, 0.2)), 0.5, 8.0),
        "query_left": bell_draw(arg_keys[3], (D_OUT, RANK), RANK ** -0.5, 0.375, ((0, 32),)),
        "query_right": bell_draw(arg_keys[4], (D_IN, RANK), 1.0, 6.0, ((0, 16),)),
        "train_left": bell_draw(arg_keys[5], (D_OUT, TRAIN), D_OUT ** -0.5, 0.046875, ((0, 32),)),
        "train_right": bell_draw(arg_keys[6], (D_IN, TRAIN), D_IN ** -0.5, 0.046875, ((0, 16),)),
    }


def dot_first(left, right):
    return lax.dot_general(left, right, (((0,), (0,)), ((), ())), precision=lax.Precision.HIGHEST, preferred_element_type=jnp.float32)


def dot_last(left, right):
    return lax.dot_general(left, right, (((1,), (1,)), ((), ())), precision=lax.Precision.HIGHEST, preferred_element_type=jnp.float32)


def reference(basis_out, basis_in, eig_damped, query_left, query_right, train_left, train_right):
    rot_left = dot_first(basis_out, query_left.astype(jnp.float32))
    rot_right = dot_first(basis_in, query_right.astype(jnp.float32))
    rot_train = dot_first(basis_in, train_right.astype(jnp.float32))

    def one_block(index):
        first = (index * 256).astype(jnp.int32)
        left_rows = lax.dynamic_slice_in_dim(rot_left, first, 256, 0)
        eigen_rows = lax.dynamic_slice_in_dim(eig_damped, first, 256, 0)
        precond = dot_last(left_rows, rot_right) / eigen_rows
        return jnp.dot(precond, rot_train, precision=lax.Precision.HIGHEST, preferred_element_type=jnp.float32)

    applied = lax.map(one_block, jnp.arange(D_OUT // 256, dtype=jnp.int32)).reshape(D_OUT, TRAIN)
    response = jnp.dot(basis_out, applied, precision=lax.Precision.HIGHEST, preferred_element_type=jnp.float32)
    scores = jnp.sum(train_left.astype(jnp.float32) * response, axis=0)
    return response, scores
```

```python
import jax
import jax.numpy as jnp
from jax import lax
from jax.sharding import PartitionSpec as P

SPAN = 240.0


def dot(left, right, contract):
    return lax.dot_general(
        left,
        right,
        (contract, ((), ())),
        precision=lax.Precision.HIGH,
        preferred_element_type=jnp.float32,
    )


def encode(x):
    peak = jnp.maximum(jnp.max(jnp.abs(x), axis=-2, keepdims=True), 1e-30)
    size = jnp.exp2(jnp.abs(x) * (SPAN / peak) - SPAN / 2)
    return jnp.where(x < 0, -size, size).astype(jnp.bfloat16), peak


def decode(code, peak):
    code = code.astype(jnp.float32)
    size = (jnp.log2(jnp.abs(code)) + SPAN / 2) * (peak / SPAN)
    return jnp.where(code < 0, -size, size)


def swap(x, axis, devices, bit):
    pairs = [(i, i ^ (1 << bit)) for i in range(devices)]
    return lax.ppermute(x, axis, pairs)


def halving_sum(x, axis, devices, order):
    bits = devices.bit_length() - 1
    me = lax.axis_index(axis)
    x = x.reshape((2,) * bits + (x.shape[0] // devices, x.shape[1]))
    left = list(range(bits - 1, -1, -1))
    for bit in order:
        place = left.index(bit)
        mine = (me >> bit) & 1
        keep = lax.dynamic_index_in_dim(x, mine, place, keepdims=False)
        send = lax.dynamic_index_in_dim(x, 1 - mine, place, keepdims=False)
        code, peak = encode(send)
        x = keep + decode(swap(code, axis, devices, bit), swap(peak, axis, devices, bit))
        left.remove(bit)
    return x


def gather(x, axis, devices):
    code, peak = encode(x)
    code = lax.all_gather(code, axis, axis=0, tiled=False)
    peak = lax.all_gather(peak, axis, axis=0, tiled=False)
    return decode(code, peak).reshape(devices * x.shape[0], x.shape[1])


def make_body(rows, cols):
    bits = cols.bit_length() - 1
    orders = [list(range(bits)), [b ^ 1 if (b ^ 1) < bits else b for b in range(bits)]]

    def body(basis_out, basis_in, eig_damped, query_left, query_right, train_left, train_right):
        rank = query_right.shape[1]
        joined = jnp.concatenate([query_right, train_right], axis=1).astype(jnp.float32)
        half = joined.shape[1] // 2
        shares = []
        for k in range(2):
            part = dot(basis_in, joined[:, k * half : (k + 1) * half], ((0,), (0,)))
            shares.append(halving_sum(part, "col", cols, orders[k]))
        share = jnp.concatenate(shares, axis=1)
        left_all = lax.all_gather(query_left, "col", axis=0, tiled=True)
        rot_left = lax.psum(dot(basis_out, left_all.astype(jnp.float32), ((0,), (0,))), "row")
        rot_right = gather(share[:, :rank], "col", cols)
        rot_train = gather(share[:, rank:], "col", cols)
        precond = dot(rot_left, rot_right, ((1,), (1,))) / eig_damped
        applied = lax.psum(dot(precond, rot_train, ((1,), (0,))), "row")
        half = applied.shape[1] // 2
        pieces = []
        for k in range(2):
            part = dot(basis_out, applied[:, k * half : (k + 1) * half], ((1,), (0,)))
            pieces.append(halving_sum(part, "col", cols, orders[k]))
        response = jnp.concatenate(pieces, axis=1)
        scores = jnp.sum(train_left.astype(jnp.float32) * response, axis=0)
        for bit in range(bits):
            scores = scores + swap(scores, "col", cols, bit)
        for bit in range(rows.bit_length() - 1):
            scores = scores + swap(scores, "row", rows, bit)
        return response, scores

    return body


def solution(mesh):
    return jax.shard_map(
        make_body(mesh.shape["row"], mesh.shape["col"]),
        mesh=mesh,
        in_specs=(
            P("row", "col"),
            P("col", "row"),
            P("col", "row"),
            P(("row", "col"), None),
            P("col", None),
            P(("row", "col"), None),
            P("col", None),
        ),
        out_specs=(P(("row", "col"), None), P()),
        check_vma=False,
    )
```
